512 devices in a mesh: dpa: 16 (over x, y_hi, core), dpb: 32 (over z, y_lo).
Axes of the slice: x: 4, y: 8 (y_hi: 2, y_lo: 4; y = y_hi * 4 + y_lo), z: 8, core: 2. Of those that a mesh axis runs over, the one named last changes fastest.
Arguments:
- activations: bfloat16 [262144, 640], P(('dpa', 'dpb')), may hold values from -6 to 6
- upstream: bfloat16 [262144, 640], P(('dpa', 'dpb')), may hold values from -6 to 6
- norm_gain: float32 [1, 640], replicated, may hold values from -0.5 to 0.5
- weight_shards: bfloat16 [1, 1966080], P(None, 'dpa'), may hold values from -0.25 to 0.25
- master: float32 [1, 1966080], P(None, ('dpa', 'dpb')), may hold values from -0.25 to 0.25
- moment_one: float32 [1, 1966080], P(None, ('dpa', 'dpb')), may hold values from -6 to 6
- moment_two: float32 [1, 1966080], P(None, ('dpa', 'dpb')), may hold values from 1 to 16
Outputs:
- grad_input: bfloat16 [262144, 640], P(('dpa', 'dpb'))
- gradient: float32 [1, 1966080], P(None, ('dpa', 'dpb'))
- new_weights: bfloat16 [1, 1966080], P(None, 'dpa')
- new_master: float32 [1, 1966080], P(None, ('dpa', 'dpb'))
- new_moment_one: float32 [1, 1966080], P(None, ('dpa', 'dpb'))
- new_moment_two: float32 [1, 1966080], P(None, ('dpa', 'dpb'))
The draws below stay inside these ranges and needn't reach their ends.
All inputs are finite; a program needn't handle non-finite values.
Results may differ from the reference program's by a relative error of at most 0.02.
Values may be sent and summed in bfloat16 or wider, within the bound.
A program may use at most 64 MiB of HBM per device.

```python
import math
import jax
import jax.numpy as jnp
from jax import lax

D = 640
FF_WIN = 1024
LAYERS = 1
TOK_DEV = 512
TOKENS = 262144
NPAR = 1966080
N_DPA = 16
N_DPB = 32


def levels(rng, dims, cuts, smallest, high):
    factor_of, own = 1.0, jax.random.fold_in(rng, 6)
    for position, parts in cuts:
        steps = jnp.exp(jax.random.uniform(jax.random.fold_in(own, position), (parts,), jnp.float32, smallest / len(cuts), high / len(cuts)))
        factor_of = factor_of * jnp.repeat(steps, dims[position] // parts).reshape([-1 if axis == position else 1 for axis in range(len(dims))])
    return factor_of


def centred(stream_key, extent, scale, most, cuts=(), held_as=jnp.bfloat16):
    entries = scale * jax.random.normal(stream_key, extent, jnp.float32)
    if cuts:
        entries = entries * levels(stream_key, extent, cuts, -0.22, 0.18)
    return jnp.clip(entries, -most, most).astype(held_as)


def setup_inputs(seed: int = 0) -> dict:
    splits = jax.random.split(jax.random.key(seed), 8)
    return {
        "activations": centred(splits[0], (TOKENS, D), 1.0, 6.0, ((0, 512),)),
        "upstream": centred(splits[1], (TOKENS, D), 1.0, 6.0, ((0, 512),)),
        "norm_gain": jnp.clip(jax.random.uniform(splits[2], (LAYERS, D), jnp.float32, -0.5, 0.5), -0.5, 0.5),
        "weight_shards": centred(splits[3], (LAYERS, NPAR), 480 ** -0.5, 0.25, ((1, 16),)),
        "master": centred(splits[4], (LAYERS, NPAR), 480 ** -0.5, 0.25, ((1, 512),), jnp.float32),
        "moment_one": centred(splits[5], (LAYERS, NPAR), 1.0, 6.0, ((1, 512),), jnp.float32),
        "moment_two": jnp.clip(jnp.exp(math.log(16.0) - 2.7725887 * jax.random.uniform(splits[6], (LAYERS, NPAR), jnp.float32) ** levels(splits[6], (LAYERS, NPAR), ((1, 512),), -0.2, 0.2)), 1.0, 16.0),
    }


def forward_layer(inputs, packed, gain):
    hidden_count = packed.shape[0] // 3
    residual = inputs.astype(jnp.float32)
    inv_rms = lax.rsqrt(lax.optimization_barrier(jnp.mean(residual * residual, axis=-1, keepdims=True)) + 1e-06)
    normed = residual * inv_rms
    gain_row = 1.0 + gain
    hidden_in = (normed * gain_row).astype(jnp.bfloat16)
    projected = lax.dot_general(hidden_in, packed[:2 * hidden_count], (((1,), (1,)), ((), ())), preferred_element_type=jnp.float32)
    gate_pre = projected[:, :hidden_count]
    up_pre = projected[:, hidden_count:]
    mixed = (jax.nn.gelu(gate_pre, approximate=True) * up_pre).astype(jnp.bfloat16)
    branch = jnp.dot(mixed, packed[2 * hidden_count:], preferred_element_type=jnp.float32)
    return (residual + branch).astype(jnp.bfloat16)

def backward_layer(inputs, packed, gain, cotangent):
    hidden_count = packed.shape[0] // 3
    residual = inputs.astype(jnp.float32)
    inv_rms = lax.rsqrt(lax.optimization_barrier(jnp.mean(residual * residual, axis=-1, keepdims=True)) + 1e-06)
    normed = residual * inv_rms
    gain_row = 1.0 + gain
    hidden_in = (normed * gain_row).astype(jnp.bfloat16)
    projected = lax.dot_general(hidden_in, packed[:2 * hidden_count], (((1,), (1,)), ((), ())), preferred_element_type=jnp.float32)
    gate_pre = projected[:, :hidden_count]
    up_pre = projected[:, hidden_count:]
    activated, pullback = jax.vjp(lambda values: jax.nn.gelu(values, approximate=True), gate_pre)
    mixed = (activated * up_pre).astype(jnp.bfloat16)
    out_rows = packed[2 * hidden_count:]
    d_mixed = lax.dot_general(cotangent, out_rows, (((1,), (1,)), ((), ())), preferred_element_type=jnp.float32)
    grad_out = lax.dot_general(mixed, cotangent, (((0,), (0,)), ((), ())), preferred_element_type=jnp.float32)
    d_gate = pullback(d_mixed * up_pre)[0]
    d_up = d_mixed * activated
    d_projected = jnp.concatenate([d_gate, d_up], axis=1).astype(jnp.bfloat16)
    grad_in = lax.dot_general(d_projected, hidden_in, (((0,), (0,)), ((), ())), preferred_element_type=jnp.float32)
    d_hidden = jnp.dot(d_projected, packed[:2 * hidden_count], preferred_element_type=jnp.float32)
    d_normed = d_hidden * gain_row
    passed = cotangent.astype(jnp.float32) + inv_rms * (d_normed - normed * lax.optimization_barrier(jnp.mean(d_normed * normed, axis=-1, keepdims=True)))
    gradient = jnp.concatenate([grad_in, grad_out], axis=0).reshape(-1)
    return (passed.astype(jnp.bfloat16), gradient)

def device_pass(packed_all, gains, block_inputs, block_upstream):
    layer_count = packed_all.shape[0]
    inputs_list = [block_inputs]
    for layer_no in range(layer_count - 1):
        inputs_list.append(forward_layer(inputs_list[-1], packed_all[layer_no], gains[layer_no]))
    cotangent = block_upstream
    gradients = [None] * layer_count
    for layer_no in reversed(range(layer_count)):
        cotangent, gradients[layer_no] = backward_layer(inputs_list[layer_no], packed_all[layer_no], gains[layer_no], cotangent)
    return (cotangent, jnp.stack(gradients))

def reference(activations, upstream, norm_gain, weight_shards, master, moment_one, moment_two):
    devices = N_DPA * N_DPB
    packed_all = weight_shards.reshape(LAYERS, 3 * FF_WIN, D)
    blocks_in = activations.reshape(devices, TOK_DEV, D)
    blocks_up = upstream.reshape(devices, TOK_DEV, D)

    def visit(summed, pieces):
        cotangent, gradients = device_pass(packed_all, norm_gain, pieces[0], pieces[1])
        rounded = lax.optimization_barrier(gradients.astype(jnp.bfloat16)).astype(jnp.float32)
        return (summed + rounded, cotangent)
    summed, cotangents = lax.scan(visit, jnp.zeros((LAYERS, NPAR), jnp.float32), (blocks_in, blocks_up))
    gradient = summed / devices
    new_moment_one = 0.9 * moment_one + 0.1 * gradient
    new_moment_two = 0.95 * moment_two + 0.05 * gradient * gradient
    new_master = master - 0.01 * (new_moment_one / (jnp.sqrt(new_moment_two) + 1e-08) + 0.1 * master)
    new_weights = new_master.astype(jnp.bfloat16)
    grad_input = cotangents.reshape(TOKENS, D)
    return (grad_input, gradient, new_weights, new_master, new_moment_one, new_moment_two)
```

```python
import math

import jax
import jax.numpy as jnp
from jax import lax
from jax.experimental import pallas as pl
from jax.experimental.pallas import tpu as pltpu
from jax.sharding import PartitionSpec as P

BF16 = jnp.bfloat16
F32 = jnp.float32
MESH = pl.DeviceIdType.MESH

D = 640
TOK = 512
NX, NY, NZ, NQ = 4, 8, 8, 4
BLK = 64
COLS = ((0, 256), (256, 256), (512, 128))

NT = (((1,), (1,)), ((), ()))
TN = (((0,), (0,)), ((), ()))

GELU_K = math.sqrt(2.0 / math.pi)


def mesh_kernel(
    act, up, gain, wsh, mas, mo1, mo2,
    gin_o, grad_o, nw_o, nm_o, n1_o, n2_o,
    xin, cin, hc, wt, pt, g4, s2, xr, yr, tsum, zs, zb, zr, nb, dh, dhr, invr,
    act_s, act_r, a1_s, a1_r, ya_s, ya_r, xa_s, xa_r, rl_s, rl_r, xg_s, xg_r, yg_s, yg_r,
    zg_s, zg_r, dh_s, dh_r, nw_s, nw_r,
):
    a = lax.axis_index("dpa")
    b = lax.axis_index("dpb")
    x, yh, c = a // 4, (a // 2) % 2, a % 2
    z, q = b // 4, b % 4
    y = yh * 4 + q

    def dev(dx=0, dy=0, z_to=None, y_to=None, c_to=None):
        xt = (x + dx + NX) % NX
        yt = (y + dy + NY) % NY if y_to is None else y_to
        zt = z if z_to is None else z_to
        ct = c if c_to is None else c_to
        return {"dpa": (xt * 2 + yt // 4) * 2 + ct, "dpb": zt * 4 + yt % 4}

    def copy(src, dst, s, r, to):
        return pltpu.make_async_remote_copy(
            src_ref=src, dst_ref=dst, send_sem=s, recv_sem=r, device_id=to, device_id_type=MESH
        )

    barrier = pltpu.get_barrier_semaphore()
    peers = [dev(c_to=1 - c), dev(dx=1), dev(dx=-1)]
    peers += [dev(dy=d) for d in range(1, NY)]
    peers += [dev(z_to=(z + d) % NZ) for d in range(1, NZ)]
    for to in peers:
        pl.semaphore_signal(barrier, inc=1, device_id=to, device_id_type=MESH)

    mine = pl.multiple_of(c * TOK, TOK)
    own_t = 3 * (2 * x + yh)
    xin[pl.ds(mine, TOK), :] = act[...]
    cin[pl.ds(mine, TOK), :] = up[...]
    wt[own_t + c] = wsh[0]
    wt[own_t + c + 1] = wsh[2]
    pl.semaphore_wait(barrier, len(peers))

    other = dev(c_to=1 - c)
    a1 = copy(wsh.at[1], wt.at[own_t + 2 * c], a1_s, a1_r, other)
    a1.start()
    acts = [
        copy(ref.at[pl.ds(mine, TOK)], ref.at[pl.ds(mine, TOK)], act_s.at[i], act_r.at[i], other)
        for i, ref in enumerate((xin, cin))
    ]
    for cp in acts:
        cp.start()
    a1.wait()

    def shard(xx, hh):
        return wt.at[pl.ds(3 * (2 * ((xx + NX) % NX) + hh), 3)]

    def shard_part(xx, hh, start, n):
        return wt.at[pl.ds(3 * (2 * ((xx + NX) % NX) + hh) + start, n)]

    left, right = dev(dx=-1), dev(dx=1)
    x_copies = []

    def x_share(hh, k):
        for j, to in enumerate((right, left)):
            cp = copy(shard(x, hh), shard(x, hh), xa_s.at[k, j], xa_r.at[k, j], to)
            cp.start()
            x_copies.append(cp)

    def x_forward(hh, k):
        cut = 2 if k == 0 else 1
        copy(shard(x - 1, hh), shard(x - 1, hh), xa_s.at[k, 0], xa_r.at[k, 0], right).wait_recv()
        part = shard_part(x - 1, hh, 0, cut)
        cp = copy(part, part, xa_s.at[k, 2], xa_r.at[k, 2], right)
        cp.start()
        x_copies.append(cp)
        copy(shard(x + 1, hh), shard(x + 1, hh), xa_s.at[k, 1], xa_r.at[k, 1], left).wait_recv()
        part = shard_part(x + 1, hh, cut, 3 - cut)
        cp = copy(part, part, xa_s.at[k, 3], xa_r.at[k, 3], left)
        cp.start()
        x_copies.append(cp)

    def x_finish(hh, k):
        cut = 2 if k == 0 else 1
        part = shard_part(x + 2, hh, 0, cut)
        copy(part, part, xa_s.at[k, 2], xa_r.at[k, 2], right).wait_recv()
        part = shard_part(x + 2, hh, cut, 3 - cut)
        copy(part, part, xa_s.at[k, 3], xa_r.at[k, 3], left).wait_recv()

    x_share(yh, 0)
    sign = jnp.where(q == 0, -1, 1)
    edge = (q == 0) | (q == NQ - 1)
    y_copies = [
        copy(shard(x, yh), shard(x, yh), ya_s.at[i], ya_r, dev(dy=sign * (i + 1))) for i in range(2)
    ]

    @pl.when(edge)
    def _():
        for cp in y_copies:
            cp.start()

    def norm(t0):
        def step(i, _):
            rows = pl.ds(pl.multiple_of(t0 + i * 128, 128), 128)
            v = xin[rows, :].astype(F32)
            s = lax.rsqrt(jnp.mean(v * v, axis=-1, keepdims=True) + 1e-6)
            invr[rows, :] = jnp.broadcast_to(s, (128, 128))
            hc[0, rows, :] = (v * s * (1.0 + gain[...])).astype(BF16)
            hc[1, rows, :] = cin[rows, :]
            return 0

        lax.fori_loop(0, TOK // 128, step, 0)

    norm(mine)
    x_forward(yh, 0)
    copy(shard(x, 1 - yh), shard(x, 1 - yh), ya_s.at[0], ya_r, right).wait_recv()
    x_share(1 - yh, 1)
    theirs = pl.multiple_of((1 - c) * TOK, TOK)
    for cp, ref in zip(acts, (xin, cin)):
        cp.wait()
    norm(theirs)
    x_forward(1 - yh, 1)
    x_finish(yh, 0)
    x_finish(1 - yh, 1)
    for cp in x_copies:
        cp.wait_send()

    @pl.when(edge)
    def _():
        for cp in y_copies:
            cp.wait_send()

    def hidden(i, _):
        u, t = i // 4, i % 4
        toks = pl.ds(pl.multiple_of(t * 256, 256), 256)
        hb, cb = hc[0, toks, :], hc[1, toks, :]

        def rows(kind):
            return wt[pl.ds(8 * kind + 4 * u, 4)].reshape(256, D)

        pa = lax.dot_general(rows(0), hb, NT, preferred_element_type=F32)
        pb = lax.dot_general(rows(1), hb, NT, preferred_element_type=F32)
        dz = lax.dot_general(rows(2), cb, NT, preferred_element_type=F32)
        sq = pa * pa
        th = jnp.tanh(GELU_K * (pa + 0.044715 * (sq * pa)))
        half = 0.5 * (1.0 + th)
        gelu = pa * half
        slope = half + (0.5 * GELU_K) * pa * (1.0 - th * th) * (1.0 + (3 * 0.044715) * sq)
        for kind, val in enumerate((slope * (dz * pb), dz * gelu, gelu * pb)):
            at = pl.ds(pl.multiple_of(512 * kind + 256 * u, 256), 256)
            pt[at, toks] = val.astype(BF16)
        return 0

    lax.fori_loop(0, 8, hidden, 0)

    relocs = []

    def grad_rows(k, dx):
        xt = (x + dx) % NX
        for i in range(3):
            n = 3 * xt + i
            val = jnp.dot(
                pt[pl.ds(pl.multiple_of(128 * n, 128), 128), :],
                hc[jnp.where(n < 8, 0, 1)],
                preferred_element_type=F32,
            ).astype(BF16)
            for e in range(2):
                m, j = divmod(2 * i + e, 3)
                slot = jnp.where(c == 0, (0, 2, 3)[j], (3, 0, 2)[j])
                g4[2 * xt + m, slot] = val[64 * e : 64 * (e + 1)]
        cp = copy(
            g4.at[pl.ds(2 * xt, 2), 3], g4.at[pl.ds(2 * xt, 2), 1], rl_s.at[k], rl_r.at[k], other
        )
        cp.start()
        relocs.append(cp)

    def part(m, p):
        return g4.at[m, pl.ds(0, 3), :, pl.ds(COLS[p][0], COLS[p][1])]

    def xbuf(i, p):
        return xr.at[i, :, :, pl.ds(COLS[p][0], COLS[p][1])]

    x_grad = []

    def x_send(src, i, p, to):
        cp = copy(src, xbuf(i, p), xg_s.at[i, p], xg_r.at[i, p], to)
        cp.start()
        x_grad.append(cp)

    def x_wait(i, p):
        copy(xbuf(i, p), xbuf(i, p), xg_s.at[i, p], xg_r.at[i, p], right).wait_recv()

    pieces = range(len(COLS))
    far, near_r, near_l = (x + 2) % NX, (x + 1) % NX, (x + 3) % NX
    grad_rows(0, 2)
    relocs[0].wait_recv()
    for p in pieces:
        x_send(part(2 * far, p), 0, p, right)
        x_send(part(2 * far + 1, p), 1, p, left)
    grad_rows(1, 1)
    grad_rows(2, 3)
    relocs[1].wait_recv()
    relocs[2].wait_recv()
    for p in pieces:
        x_send(part(2 * near_r + 1, p), 2, p, right)
        x_send(part(2 * near_l, p), 3, p, left)
    grad_rows(3, 0)

    for p in pieces:
        cols = pl.ds(COLS[p][0], COLS[p][1])
        for i, m, to in ((0, 2 * near_r, right), (1, 2 * near_l + 1, left)):
            x_wait(i, p)
            tot = g4[m, 0:3, :, cols].astype(F32) + xr[i, :, :, cols].astype(F32)
            g4[m, 0:3, :, cols] = tot.astype(BF16)
            x_send(part(m, p), 4 + i, p, to)

    def dh_rows(t0):
        def step(i, _):
            toks = pl.ds(pl.multiple_of(t0 + i * 256, 256), 256)
            dh[toks, :] = lax.dot_general(
                pt[pl.ds(0, 1024), toks], wt[0:16].reshape(1024, D), TN, preferred_element_type=F32
            )
            return 0

        lax.fori_loop(0, 2, step, 0)

    dh_rows(theirs)
    dh_copy = copy(dh.at[pl.ds(theirs, TOK)], dhr, dh_s, dh_r, other)
    dh_copy.start()
    dh_rows(mine)
    relocs[3].wait_recv()

    y_grad = []
    for p in pieces:
        cols = pl.ds(COLS[p][0], COLS[p][1])
        for i, (one, two) in enumerate(((4, 3), (2, 5))):
            x_wait(one, p)
            x_wait(two, p)
            tot = g4[2 * x + i, 0:3, :, cols].astype(F32) + xr[one, :, :, cols].astype(F32)
            tot = tot + xr[two, :, :, cols].astype(F32)
            s2[i, :, cols] = tot.reshape(192, COLS[p][1]).astype(BF16)
        for d in range(1, NY):
            yt = (y + d) % NY
            cp = copy(
                s2.at[yt // 4, pl.ds(pl.multiple_of(48 * (yt % 4), 16), 48), cols],
                yr.at[d, :, cols],
                yg_s.at[d, p],
                yg_r.at[d, p],
                dev(dy=d),
            )
            cp.start()
            y_grad.append(cp)

    dh_copy.wait()

    def finish_input(i, _):
        loc = pl.ds(pl.multiple_of(i * 128, 128), 128)
        rows = pl.ds(pl.multiple_of(mine + i * 128, 128), 128)
        dn = (dh[rows, :] + dhr[loc, :]) * (1.0 + gain[...])
        s = invr[rows, 0:1]
        n = xin[rows, :].astype(F32) * s
        mean = jnp.mean(dn * n, axis=-1, keepdims=True)
        gin_o[loc, :] = (cin[rows, :].astype(F32) + s * (dn - n * mean)).astype(BF16)
        return 0

    lax.fori_loop(0, TOK // 128, finish_input, 0)

    own = pl.ds(pl.multiple_of(48 * q, 16), 48)
    for p in pieces:
        cols = pl.ds(COLS[p][0], COLS[p][1])
        tot = s2[yh, own, cols].astype(F32)
        for d in range(1, NY):
            copy(
                yr.at[d, :, cols], yr.at[d, :, cols], yg_s.at[d, p], yg_r.at[d, p], right
            ).wait_recv()
            tot = tot + yr[d, :, cols].astype(F32)
        tsum[:, cols] = tot

    zs[...] = jnp.zeros_like(zs)
    for r in range(48):
        blk, jj = divmod(r, 6)
        for w in range(5):
            zs[blk, pl.ds(5 * jj + w, 1), :] = tsum[pl.ds(r, 1), pl.ds(128 * w, 128)]
    zb[...] = zs[...].astype(BF16)
    for e in range(2):
        for qt in range(NQ):
            zt = 2 * q + e
            self = (zt == z) & (q == qt)

            @pl.when(jnp.logical_not(self))
            def _():
                copy(
                    zb.at[e * 4 + qt], zr.at[z], zg_s.at[e * 4 + qt], zg_r.at[z],
                    dev(z_to=zt, y_to=yh * 4 + qt),
                ).start()

            @pl.when(self)
            def _():
                zr[z] = zb[e * 4 + qt]

    tot = jnp.zeros((32, 128), F32)
    for zf in range(NZ):
        self = (z // 2 == q) & (z == zf)

        @pl.when(jnp.logical_not(self))
        def _():
            copy(zr.at[zf], zr.at[zf], zg_s.at[0], zg_r.at[zf], right).wait_recv()

        tot = tot + zr[zf].astype(F32)

    grad = tot[0:30] * (1.0 / 512.0)
    n1 = 0.9 * mo1[...] + 0.1 * grad
    n2 = 0.95 * mo2[...] + 0.05 * grad * grad
    nm = mas[...] - 0.01 * (n1 / (jnp.sqrt(n2) + 1e-8) + 0.1 * mas[...])
    nb[pl.ds(0, 30), :] = nm
    nb[pl.ds(30, 2), :] = jnp.zeros((2, 128), F32)
    nw_o[b] = nb[...].astype(BF16)
    new = []
    for dz in range(NZ):
        for dq in range(NQ):
            if dz or dq:
                zt = (z + dz) % NZ
                cp = copy(
                    nw_o.at[b], nw_o.at[b], nw_s.at[dz, dq], nw_r.at[dz, dq],
                    dev(z_to=zt, y_to=yh * 4 + (q + dq) % NQ),
                )
                cp.start()
                new.append(cp)
    grad_o[...] = grad
    n1_o[...] = n1
    n2_o[...] = n2
    nm_o[...] = nm

    for cp in relocs + x_grad + y_grad:
        cp.wait_send()
    for e in range(2):
        for qt in range(NQ):
            self = (2 * q + e == z) & (q == qt)

            @pl.when(jnp.logical_not(self))
            def _():
                copy(zb.at[e * 4 + qt], zr.at[z], zg_s.at[e * 4 + qt], zg_r.at[z], right).wait_send()

    for dz in range(NZ):
        for dq in range(NQ):
            if dz or dq:
                bf = ((z - dz + NZ) % NZ) * 4 + (q - dq + NQ) % NQ
                copy(nw_o.at[bf], nw_o.at[bf], nw_s.at[dz, dq], nw_r.at[dz, dq], right).wait_recv()
    for cp in new:
        cp.wait_send()


def shards(activations, upstream, norm_gain, weight_shards, master, moment_one, moment_two):
    vm = pl.BlockSpec(memory_space=pltpu.VMEM)
    dma = pltpu.SemaphoreType.DMA
    np_ = len(COLS)
    state = [v.reshape(30, 128) for v in (master, moment_one, moment_two)]
    shape = jax.ShapeDtypeStruct
    gin, grad, nw, nm, n1, n2 = pl.pallas_call(
        mesh_kernel,
        out_shape=[
            shape((TOK, D), BF16),
            shape((30, 128), F32),
            shape((32, 32, 128), BF16),
            shape((30, 128), F32),
            shape((30, 128), F32),
            shape((30, 128), F32),
        ],
        in_specs=[vm] * 7,
        out_specs=[vm] * 6,
        scratch_shapes=[
            pltpu.VMEM((2 * TOK, D), BF16),
            pltpu.VMEM((2 * TOK, D), BF16),
            pltpu.VMEM((2, 2 * TOK, D), BF16),
            pltpu.VMEM((24, BLK, D), BF16),
            pltpu.VMEM((1536, 2 * TOK), BF16),
            pltpu.VMEM((8, 4, BLK, D), BF16),
            pltpu.VMEM((2, 192, D), BF16),
            pltpu.VMEM((6, 3, BLK, D), BF16),
            pltpu.VMEM((NY, 48, D), BF16),
            pltpu.VMEM((48, D), F32),
            pltpu.VMEM((8, 32, 128), F32),
            pltpu.VMEM((8, 32, 128), BF16),
            pltpu.VMEM((NZ, 32, 128), BF16),
            pltpu.VMEM((32, 128), F32),
            pltpu.VMEM((2 * TOK, D), F32),
            pltpu.VMEM((TOK, D), F32),
            pltpu.VMEM((2 * TOK, 128), F32),
            dma((2,)), dma((2,)),
            dma, dma,
            dma((2,)), dma,
            dma((2, 4)), dma((2, 4)),
            dma((4,)), dma((4,)),
            dma((6, np_)), dma((6, np_)),
            dma((NY, np_)), dma((NY, np_)),
            dma((8,)), dma((NZ,)),
            dma, dma,
            dma((NZ, NQ)), dma((NZ, NQ)),
        ],
        compiler_params=pltpu.CompilerParams(
            collective_id=0, has_side_effects=True, vmem_limit_bytes=56 * 1024 * 1024
        ),
        name="ffn_backward_adam",
    )(activations, upstream, norm_gain, weight_shards.reshape(3, BLK, D), *state)
    flat = lambda v: v.reshape(1, 3840)
    return (
        gin,
        flat(grad),
        nw[:, :30].reshape(1, 32 * 3840),
        flat(nm),
        flat(n1),
        flat(n2),
    )


def solution(mesh):
    own = P(None, ("dpa", "dpb"))
    rows = P(("dpa", "dpb"), None)
    return jax.shard_map(
        shards,
        mesh=mesh,
        in_specs=(rows, rows, P(), P(None, "dpa"), own, own, own),
        out_specs=(rows, own, P(None, "dpa"), own, own, own),
        check_vma=False,
    )
```

```python
import math

import jax
import jax.numpy as jnp
from jax import lax
from jax.experimental import pallas as pl
from jax.experimental.pallas import tpu as pltpu
from jax.sharding import PartitionSpec as P

BF16 = jnp.bfloat16
F32 = jnp.float32
MESH = pl.DeviceIdType.MESH

D = 640
TOK = 512
NX, NY, NZ, NQ = 4, 8, 8, 4
BLK = 64
COLS = ((0, 256), (256, 256), (512, 128))

NT = (((1,), (1,)), ((), ()))
TN = (((0,), (0,)), ((), ()))

GELU_K = math.sqrt(2.0 / math.pi)


def mesh_kernel(
    act, up, gain, wflat, mas, mo1, mo2,
    gin_o, grad_o, nw_o, nm_o, n1_o, n2_o,
    wf, wsh, state, nwr, xin, cin, hc, w2, pt, g4, s2, xr, yr, tsum, zs, zb, zr, nb, dh, dhr, invr,
    act_s, act_r, a1_s, a1_r, ya_s, ya_r, xa_s, xa_r, xo_s, xo_r, za_s, za_r, rl_s, rl_r, xg_s, xg_r, yg_s, yg_r,
    zg_s, zg_r, dh_s, dh_r, nw_s, nw_r,
):
    a = lax.axis_index("dpa")
    b = lax.axis_index("dpb")
    x, yh, c = a // 4, (a // 2) % 2, a % 2
    z, q = b // 4, b % 4
    y = yh * 4 + q

    def dev(dx=0, dy=0, z_to=None, y_to=None, c_to=None):
        xt = (x + dx + NX) % NX
        yt = (y + dy + NY) % NY if y_to is None else y_to
        zt = z if z_to is None else z_to
        ct = c if c_to is None else c_to
        return {"dpa": (xt * 2 + yt // 4) * 2 + ct, "dpb": zt * 4 + yt % 4}

    def copy(src, dst, s, r, to):
        return pltpu.make_async_remote_copy(
            src_ref=src, dst_ref=dst, send_sem=s, recv_sem=r, device_id=to, device_id_type=MESH
        )

    barrier = pltpu.get_barrier_semaphore()
    peers = [dev(c_to=1 - c), dev(dx=1), dev(dx=-1)]
    peers += [dev(dy=d) for d in range(1, NY)]
    peers += [dev(z_to=(z + d) % NZ) for d in range(1, NZ)]
    for to in peers:
        pl.semaphore_signal(barrier, inc=1, device_id=to, device_id_type=MESH)

    mine = pl.multiple_of(c * TOK, TOK)
    theirs = pl.multiple_of((1 - c) * TOK, TOK)
    own_t = 3 * (2 * x + yh)

    def blocks(t, n=1):
        return pl.ds(pl.multiple_of(BLK * t, BLK), BLK * n)

    xin[pl.ds(mine, TOK), :] = act[...]
    cin[pl.ds(mine, TOK), :] = up[...]
    for r in range(3 * BLK):
        wf[pl.ds(r, 1), :] = wflat[:, pl.ds(D * r, D)].astype(F32)
    w2[blocks(own_t + c)] = wf[0:64].astype(BF16)
    wsh[...] = wf[64:128].astype(BF16)
    w2[blocks(own_t + c + 1)] = wf[128:192].astype(BF16)
    for i, ref in enumerate((mas, mo1, mo2)):
        for r in range(30):
            state[i, pl.ds(r, 1), :] = ref[:, pl.ds(128 * r, 128)]
    pl.semaphore_wait(barrier, len(peers))

    other = dev(c_to=1 - c)
    a1 = copy(wsh, w2.at[blocks(own_t + 2 * c)], a1_s, a1_r, other)
    a1.start()
    acts = [
        copy(ref.at[pl.ds(mine, TOK)], ref.at[pl.ds(mine, TOK)], act_s.at[i], act_r.at[i], other)
        for i, ref in enumerate((xin, cin))
    ]
    for cp in acts:
        cp.start()
    a1.wait()

    def shard(xx, hh):
        return shard_part(xx, hh, 0, 3)

    def shard_part(xx, hh, start, n):
        at = 192 * (2 * ((xx + NX) % NX) + hh) + BLK * start
        return w2.at[pl.ds(pl.multiple_of(at, BLK), BLK * n)]

    left, right = dev(dx=-1), dev(dx=1)
    x_copies = []

    def x_share(hh, k):
        for j, to in enumerate((right, left)):
            cp = copy(shard(x, hh), shard(x, hh), xa_s.at[k, j], xa_r.at[k, j], to)
            cp.start()
            x_copies.append(cp)

    def x_forward(hh, k):
        cut = 2 if k == 0 else 1
        copy(shard(x - 1, hh), shard(x - 1, hh), xa_s.at[k, 0], xa_r.at[k, 0], right).wait_recv()
        part = shard_part(x - 1, hh, 0, cut)
        cp = copy(part, part, xa_s.at[k, 2], xa_r.at[k, 2], right)
        cp.start()
        x_copies.append(cp)
        copy(shard(x + 1, hh), shard(x + 1, hh), xa_s.at[k, 1], xa_r.at[k, 1], left).wait_recv()
        part = shard_part(x + 1, hh, cut, 3 - cut)
        cp = copy(part, part, xa_s.at[k, 3], xa_r.at[k, 3], left)
        cp.start()
        x_copies.append(cp)

    def x_finish(hh, k):
        cut = 2 if k == 0 else 1
        part = shard_part(x + 2, hh, 0, cut)
        copy(part, part, xa_s.at[k, 2], xa_r.at[k, 2], right).wait_recv()
        part = shard_part(x + 2, hh, cut, 3 - cut)
        copy(part, part, xa_s.at[k, 3], xa_r.at[k, 3], left).wait_recv()

    x_share(yh, 0)
    sign = jnp.where(q == 0, -1, 1)
    edge = (q == 0) | (q == NQ - 1)
    odd = z % 2
    oh = 1 - yh

    def piece(xx, hh, h, k):
        start = 192 * (2 * ((xx + NX) % NX) + hh) + 96 * h + 48 * k
        return w2.at[pl.ds(pl.multiple_of(start, 16), 48)]

    def send_piece(ref, s, r, to):
        cp = copy(ref, ref, s, r, to)
        cp.start()
        x_copies.append(cp)

    y_copies = []
    for k in range(2):
        for j in (1, 0):
            ref = piece(x, yh, odd, k)
            y_copies.append(copy(ref, ref, ya_s.at[k, j], ya_r.at[k], dev(dy=sign * (j + 1))))

    @pl.when(edge)
    def _():
        for cp in y_copies:
            cp.start()

    up_z, down_z = dev(z_to=(z + 1) % NZ), dev(z_to=(z + NZ - 1) % NZ)

    def z_send(dx, k):
        ref = piece(x + dx, oh, odd, k)
        send_piece(ref, za_s.at[dx, k], za_r.at[dx, k], (up_z, down_z)[k])

    def norm(t0):
        def step(i, _):
            rows = pl.ds(pl.multiple_of(t0 + i * 128, 128), 128)
            v = xin[rows, :].astype(F32)
            s = lax.rsqrt(jnp.mean(v * v, axis=-1, keepdims=True) + 1e-6)
            invr[rows, :] = jnp.broadcast_to(s, (128, 128))
            hc[0, rows, :] = (v * s * (1.0 + gain[...])).astype(BF16)
            hc[1, rows, :] = cin[rows, :]
            return 0

        lax.fori_loop(0, TOK // 128, step, 0)

    norm(mine)
    for k in range(2):
        ref = piece(x, oh, odd, k)
        copy(ref, ref, ya_s.at[k, 0], ya_r.at[k], right).wait_recv()
        for j, to in enumerate((right, left)):
            send_piece(ref, xo_s.at[k, j], xo_r.at[k, j], to)
        z_send(0, k)
    x_forward(yh, 0)
    for cp, ref in zip(acts, (xin, cin)):
        cp.wait()
    for k in range(2):
        for j, dx in enumerate((3, 1)):
            ref = piece(x + dx, oh, odd, k)
            copy(ref, ref, xo_s.at[k, j], xo_r.at[k, j], right).wait_recv()
            if j == k:
                send_piece(ref, xo_s.at[2, k], xo_r.at[2, k], (right, left)[k])
            z_send(dx, k)
    norm(theirs)
    x_finish(yh, 0)
    for k in range(2):
        ref = piece(x + 2, oh, odd, k)
        copy(ref, ref, xo_s.at[2, k], xo_r.at[2, k], right).wait_recv()
        z_send(2, k)
    for dx in (0, 3, 1, 2):
        for k in range(2):
            ref = piece(x + dx, oh, 1 - odd, k)
            copy(ref, ref, za_s.at[dx, k], za_r.at[dx, k], right).wait_recv()
    for cp in x_copies:
        cp.wait_send()

    @pl.when(edge)
    def _():
        for cp in y_copies:
            cp.wait_send()

    def hidden(i, _):
        u, t = i // 4, i % 4
        toks = pl.ds(pl.multiple_of(t * 256, 256), 256)
        hb, cb = hc[0, toks, :], hc[1, toks, :]

        def rows(kind):
            return w2[blocks(8 * kind + 4 * u, 4), :]

        pa = lax.dot_general(rows(0), hb, NT, preferred_element_type=F32)
        pb = lax.dot_general(rows(1), hb, NT, preferred_element_type=F32)
        dz = lax.dot_general(rows(2), cb, NT, preferred_element_type=F32)
        sq = pa * pa
        th = jnp.tanh(GELU_K * (pa + 0.044715 * (sq * pa)))
        half = 0.5 * (1.0 + th)
        gelu = pa * half
        slope = half + (0.5 * GELU_K) * pa * (1.0 - th * th) * (1.0 + (3 * 0.044715) * sq)
        for kind, val in enumerate((slope * (dz * pb), dz * gelu, gelu * pb)):
            at = pl.ds(pl.multiple_of(512 * kind + 256 * u, 256), 256)
            pt[at, toks] = val.astype(BF16)
        return 0

    lax.fori_loop(0, 8, hidden, 0)

    def grad_rows(dx, p):
        xt = (x + dx) % NX
        cols = pl.ds(COLS[p][0], COLS[p][1])
        for i in range(3):
            n = 3 * xt + i
            val = jnp.dot(
                pt[pl.ds(pl.multiple_of(128 * n, 128), 128), :],
                hc[jnp.where(n < 8, 0, 1), :, cols],
                preferred_element_type=F32,
            ).astype(BF16)
            for e in range(2):
                m, j = divmod(2 * i + e, 3)
                g4[2 * xt + m, j, :, cols] = val[64 * e : 64 * (e + 1)]

    def part(m, p):
        return g4.at[m, :, :, pl.ds(COLS[p][0], COLS[p][1])]

    def xbuf(i, p):
        return xr.at[i, :, :, pl.ds(COLS[p][0], COLS[p][1])]

    x_grad, relocs, y_grad = [], [], []

    def x_send(src, i, p, to):
        cp = copy(src, xbuf(i, p), xg_s.at[i, p], xg_r.at[i, p], to)
        cp.start()
        x_grad.append(cp)

    def x_wait(i, p):
        copy(xbuf(i, p), xbuf(i, p), xg_s.at[i, p], xg_r.at[i, p], right).wait_recv()

    pieces = range(len(COLS))
    far, near_r, near_l = (x + 2) % NX, (x + 1) % NX, (x + 3) % NX

    def rows_far(p):
        grad_rows(2, p)
        x_send(part(2 * far, p), 0, p, right)
        x_send(part(2 * far + 1, p), 1, p, left)

    def rows_near(p):
        grad_rows(1, p)
        x_send(part(2 * near_r + 1, p), 2, p, right)
        grad_rows(3, p)
        x_send(part(2 * near_l, p), 3, p, left)
        grad_rows(0, p)

    def x_pass(p):
        cols = pl.ds(COLS[p][0], COLS[p][1])
        for i, m, to in ((0, 2 * near_r, right), (1, 2 * near_l + 1, left)):
            x_wait(i, p)
            tot = g4[m, :, :, cols].astype(F32) + xr[i, :, :, cols].astype(F32)
            g4[m, :, :, cols] = tot.astype(BF16)
            x_send(part(m, p), 4 + i, p, to)

    def x_done(p):
        cols = pl.ds(COLS[p][0], COLS[p][1])
        for i, (one, two) in enumerate(((4, 3), (2, 5))):
            x_wait(two if i == 0 else one, p)
            x_wait(one if i == 0 else two, p)
            tot = g4[2 * x + i, :, :, cols].astype(F32) + xr[one, :, :, cols].astype(F32)
            tot = (tot + xr[two, :, :, cols].astype(F32)).astype(BF16)
            for j in range(3):
                slot = jnp.where(c == 0, (0, 2, 3)[j], (3, 0, 2)[j])
                s2[i, pl.ds(pl.multiple_of(64 * slot, 64), 64), cols] = tot[j]
        cp = copy(
            s2.at[:, pl.ds(192, 64), cols], s2.at[:, pl.ds(64, 64), cols], rl_s.at[p], rl_r.at[p], other
        )
        cp.start()
        relocs.append(cp)

    def y_start(p):
        cols = pl.ds(COLS[p][0], COLS[p][1])
        relocs[p].wait_recv()
        for d in (4, 3, 5, 2, 6, 1, 7):
            yt = (y + d) % NY
            cp = copy(
                s2.at[yt // 4, pl.ds(pl.multiple_of(48 * (yt % 4), 16), 48), cols],
                yr.at[d, :, cols],
                yg_s.at[d, p],
                yg_r.at[d, p],
                dev(dy=d),
            )
            cp.start()
            y_grad.append(cp)

    def dh_rows(t0):
        def step(i, _):
            toks = pl.ds(pl.multiple_of(t0 + i * 256, 256), 256)
            dh[toks, :] = lax.dot_general(
                pt[pl.ds(0, 1024), toks], w2[0:1024, :], TN, preferred_element_type=F32
            )
            return 0

        lax.fori_loop(0, 2, step, 0)

    last = len(COLS) - 1
    rows_far(0)
    rows_near(0)
    for p in range(1, last + 1):
        rows_far(p)
        x_pass(p - 1)
        rows_near(p)
        if p >= 2:
            x_done(p - 2)
            y_start(p - 2)
    if last >= 1:
        x_done(last - 1)
        y_start(last - 1)
    x_pass(last)
    dh_rows(theirs)
    dh_copy = copy(dh.at[pl.ds(theirs, TOK)], dhr, dh_s, dh_r, other)
    dh_copy.start()
    x_done(last)
    y_start(last)
    dh_rows(mine)

    dh_copy.wait()

    def finish_input(i, _):
        loc = pl.ds(pl.multiple_of(i * 128, 128), 128)
        rows = pl.ds(pl.multiple_of(mine + i * 128, 128), 128)
        dn = (dh[rows, :] + dhr[loc, :]) * (1.0 + gain[...])
        s = invr[rows, 0:1]
        n = xin[rows, :].astype(F32) * s
        mean = jnp.mean(dn * n, axis=-1, keepdims=True)
        gin_o[loc, :] = (cin[rows, :].astype(F32) + s * (dn - n * mean)).astype(BF16)
        return 0

    lax.fori_loop(0, TOK // 128, finish_input, 0)

    own = pl.ds(pl.multiple_of(48 * q, 16), 48)
    for p in pieces:
        cols = pl.ds(COLS[p][0], COLS[p][1])
        tot = s2[yh, own, cols].astype(F32)
        for d in range(1, NY):
            copy(
                yr.at[d, :, cols], yr.at[d, :, cols], yg_s.at[d, p], yg_r.at[d, p], right
            ).wait_recv()
            tot = tot + yr[d, :, cols].astype(F32)
        tsum[:, cols] = tot

    zs[...] = jnp.zeros_like(zs)
    for r in range(48):
        blk, jj = divmod(r, 6)
        for w in range(5):
            zs[blk, pl.ds(5 * jj + w, 1), :] = tsum[pl.ds(r, 1), pl.ds(128 * w, 128)]
    zb[...] = zs[...].astype(BF16)
    for e in range(2):
        for qt in range(NQ):
            zt = 2 * q + e
            self = (zt == z) & (q == qt)

            @pl.when(jnp.logical_not(self))
            def _():
                copy(
                    zb.at[e * 4 + qt], zr.at[z], zg_s.at[e * 4 + qt], zg_r.at[z],
                    dev(z_to=zt, y_to=yh * 4 + qt),
                ).start()

            @pl.when(self)
            def _():
                zr[z] = zb[e * 4 + qt]

    tot = jnp.zeros((32, 128), F32)
    for zf in range(NZ):
        self = (z // 2 == q) & (z == zf)

        @pl.when(jnp.logical_not(self))
        def _():
            copy(zr.at[zf], zr.at[zf], zg_s.at[0], zg_r.at[zf], right).wait_recv()

        tot = tot + zr[zf].astype(F32)

    grad = tot[0:30] * (1.0 / 512.0)
    n1 = 0.9 * state[1] + 0.1 * grad
    n2 = 0.95 * state[2] + 0.05 * grad * grad
    nm = state[0] - 0.01 * (n1 / (jnp.sqrt(n2) + 1e-8) + 0.1 * state[0])
    nb[pl.ds(0, 30), :] = nm
    nb[pl.ds(30, 2), :] = jnp.zeros((2, 128), F32)
    nwr[b] = nb[...].astype(BF16)
    new = []
    near_first = [(dz, dq) for dz in range(NZ) for dq in range(NQ) if dz or dq]
    near_first.sort(key=lambda v: (min(v[0], NZ - v[0]) + v[1], v))
    for dz, dq in near_first[::-1]:
        cp = copy(
            nwr.at[b], nwr.at[b], nw_s.at[dz, dq], nw_r.at[dz, dq],
            dev(z_to=(z + dz) % NZ, y_to=yh * 4 + (q + dq) % NQ),
        )
        cp.start()
        new.append(cp)
    for ref, val in ((grad_o, grad), (n1_o, n1), (n2_o, n2), (nm_o, nm)):
        for r in range(30):
            ref[:, pl.ds(128 * r, 128)] = val[r : r + 1]

    for cp in relocs + x_grad + y_grad:
        cp.wait_send()
    for e in range(2):
        for qt in range(NQ):
            self = (2 * q + e == z) & (q == qt)

            @pl.when(jnp.logical_not(self))
            def _():
                copy(zb.at[e * 4 + qt], zr.at[z], zg_s.at[e * 4 + qt], zg_r.at[z], right).wait_send()

    def lay_flat(i):
        rows = nwr[i].astype(F32)
        for r in range(30):
            nw_o[:, pl.ds(pl.multiple_of(3840 * i + 128 * r, 128), 128)] = rows[r : r + 1].astype(BF16)

    lay_flat(b)
    for dz, dq in near_first:
        bf = ((z - dz + NZ) % NZ) * 4 + (q - dq + NQ) % NQ
        copy(nwr.at[bf], nwr.at[bf], nw_s.at[dz, dq], nw_r.at[dz, dq], right).wait_recv()
        lay_flat(bf)
    for cp in new:
        cp.wait_send()


def shards(activations, upstream, norm_gain, weight_shards, master, moment_one, moment_two):
    vm = pl.BlockSpec(memory_space=pltpu.VMEM)
    dma = pltpu.SemaphoreType.DMA
    np_ = len(COLS)
    shape = jax.ShapeDtypeStruct
    gin, grad, nw, nm, n1, n2 = pl.pallas_call(
        mesh_kernel,
        out_shape=[
            shape((TOK, D), BF16),
            shape((1, 3840), F32),
            shape((1, 32 * 3840), BF16),
            shape((1, 3840), F32),
            shape((1, 3840), F32),
            shape((1, 3840), F32),
        ],
        in_specs=[vm] * 7,
        out_specs=[vm] * 6,
        scratch_shapes=[
            pltpu.VMEM((3 * BLK, D), F32),
            pltpu.VMEM((BLK, D), BF16),
            pltpu.VMEM((3, 30, 128), F32),
            pltpu.VMEM((32, 32, 128), BF16),
            pltpu.VMEM((2 * TOK, D), BF16),
            pltpu.VMEM((2 * TOK, D), BF16),
            pltpu.VMEM((2, 2 * TOK, D), BF16),
            pltpu.VMEM((24 * BLK, D), BF16),
            pltpu.VMEM((1536, 2 * TOK), BF16),
            pltpu.VMEM((8, 3, BLK, D), BF16),
            pltpu.VMEM((2, 256, D), BF16),
            pltpu.VMEM((6, 3, BLK, D), BF16),
            pltpu.VMEM((NY, 48, D), BF16),
            pltpu.VMEM((48, D), F32),
            pltpu.VMEM((8, 32, 128), F32),
            pltpu.VMEM((8, 32, 128), BF16),
            pltpu.VMEM((NZ, 32, 128), BF16),
            pltpu.VMEM((32, 128), F32),
            pltpu.VMEM((2 * TOK, D), F32),
            pltpu.VMEM((TOK, D), F32),
            pltpu.VMEM((2 * TOK, 128), F32),
            dma((2,)), dma((2,)),
            dma, dma,
            dma((2, 2)), dma((2,)),
            dma((1, 4)), dma((1, 4)),
            dma((3, 2)), dma((3, 2)),
            dma((NX, 2)), dma((NX, 2)),
            dma((np_,)), dma((np_,)),
            dma((6, np_)), dma((6, np_)),
            dma((NY, np_)), dma((NY, np_)),
            dma((8,)), dma((NZ,)),
            dma, dma,
            dma((NZ, NQ)), dma((NZ, NQ)),
        ],
        compiler_params=pltpu.CompilerParams(
            collective_id=0, has_side_effects=True, vmem_limit_bytes=56 * 1024 * 1024
        ),
        name="ffn_backward_adam",
    )(activations, upstream, norm_gain, weight_shards, master, moment_one, moment_two)
    return emit(gin, grad, nw, nm, n1, n2)


def emit_kernel(*refs):
    for src, dst in zip(refs[:6], refs[6:]):
        dst[...] = src[...]


def emit(*arrays):
    vm = pl.BlockSpec(memory_space=pltpu.VMEM)
    return pl.pallas_call(
        emit_kernel,
        out_shape=[jax.ShapeDtypeStruct(v.shape, v.dtype) for v in arrays],
        in_specs=[vm] * 6,
        out_specs=[vm] * 6,
        name="emit",
    )(*arrays)


def solution(mesh):
    own = P(None, ("dpa", "dpb"))
    rows = P(("dpa", "dpb"), None)
    return jax.shard_map(
        shards,
        mesh=mesh,
        in_specs=(rows, rows, P(), P(None, "dpa"), own, own, own),
        out_specs=(rows, own, P(None, "dpa"), own, own, own),
        check_vma=False,
    )
```

```python
import math

import jax
import jax.numpy as jnp
from jax import lax
from jax.experimental import pallas as pl
from jax.experimental.pallas import tpu as pltpu
from jax.sharding import PartitionSpec as P

BF16 = jnp.bfloat16
F32 = jnp.float32
MESH = pl.DeviceIdType.MESH

D = 640
TOK = 512
NX, NY, NZ, NQ = 4, 8, 8, 4
BLK = 64
COLS = ((0, 128), (128, 256), (384, 128), (512, 128))

NT = (((1,), (1,)), ((), ()))
TN = (((0,), (0,)), ((), ()))

GELU_K = math.sqrt(2.0 / math.pi)


def mesh_kernel(
    act, up, gain, wflat, mas, mo1, mo2,
    gin_o, grad_o, nw_o, nm_o, n1_o, n2_o,
    wf, wsh, state, nwr, xin, cin, hc, w2, pt, g4, s2, xr, yr, tsum, zs, zb, zr, nb, dh, dhr, invr,
    ld_s, act_s, act_r, a1_s, a1_r, ya_s, ya_r, xa_s, xa_r, xo_s, xo_r, za_s, za_r, rl_s, rl_r, xg_s, xg_r, yg_s, yg_r,
    zg_s, zg_r, dh_s, dh_r, nw_s, nw_r,
):
    a = lax.axis_index("dpa")
    b = lax.axis_index("dpb")
    x, yh, c = a // 4, (a // 2) % 2, a % 2
    z, q = b // 4, b % 4
    y = yh * 4 + q

    def dev(dx=0, dy=0, z_to=None, y_to=None, c_to=None):
        xt = (x + dx + NX) % NX
        yt = (y + dy + NY) % NY if y_to is None else y_to
        zt = z if z_to is None else z_to
        ct = c if c_to is None else c_to
        return {"dpa": (xt * 2 + yt // 4) * 2 + ct, "dpb": zt * 4 + yt % 4}

    def copy(src, dst, s, r, to):
        return pltpu.make_async_remote_copy(
            src_ref=src, dst_ref=dst, send_sem=s, recv_sem=r, device_id=to, device_id_type=MESH
        )

    barrier = pltpu.get_barrier_semaphore()
    peers = [dev(c_to=1 - c), dev(dx=1), dev(dx=-1)]
    peers += [dev(dy=d) for d in range(1, NY)]
    peers += [dev(z_to=(z + d) % NZ) for d in range(1, NZ)]
    for to in peers:
        pl.semaphore_signal(barrier, inc=1, device_id=to, device_id_type=MESH)

    mine = pl.multiple_of(c * TOK, TOK)
    theirs = pl.multiple_of((1 - c) * TOK, TOK)
    own_t = 3 * (2 * x + yh)

    def blocks(t, n=1):
        return pl.ds(pl.multiple_of(BLK * t, BLK), BLK * n)

    loads = [
        pltpu.make_async_copy(src, dst.at[pl.ds(mine, TOK)], ld_s.at[i])
        for i, (src, dst) in enumerate(((act, xin), (up, cin)))
    ]
    for cp in loads:
        cp.start()
    for r in range(3 * BLK):
        wf[pl.ds(r, 1), :] = wflat[:, pl.ds(D * r, D)].astype(F32)
    w2[blocks(own_t + c)] = wf[0:64].astype(BF16)
    wsh[...] = wf[64:128].astype(BF16)
    w2[blocks(own_t + c + 1)] = wf[128:192].astype(BF16)
    for i, ref in enumerate((mas, mo1, mo2)):
        for r in range(30):
            state[i, pl.ds(r, 1), :] = ref[:, pl.ds(128 * r, 128)]
    pl.semaphore_wait(barrier, len(peers))

    other = dev(c_to=1 - c)
    a1 = copy(wsh, w2.at[blocks(own_t + 2 * c)], a1_s, a1_r, other)
    a1.start()
    acts = [
        copy(ref.at[pl.ds(mine, TOK)], ref.at[pl.ds(mine, TOK)], act_s.at[i], act_r.at[i], other)
        for i, ref in enumerate((xin, cin))
    ]
    for cp, load in zip(acts, loads):
        load.wait()
        cp.start()
    a1.wait()

    def shard(xx, hh):
        return shard_part(xx, hh, 0, 3)

    def shard_part(xx, hh, start, n):
        at = 192 * (2 * ((xx + NX) % NX) + hh) + BLK * start
        return w2.at[pl.ds(pl.multiple_of(at, BLK), BLK * n)]

    left, right = dev(dx=-1), dev(dx=1)
    x_copies = []

    def x_share(hh, k):
        for j, to in enumerate((right, left)):
            cp = copy(shard(x, hh), shard(x, hh), xa_s.at[k, j], xa_r.at[k, j], to)
            cp.start()
            x_copies.append(cp)

    def x_forward(hh, k):
        cut = 2 if k == 0 else 1
        copy(shard(x - 1, hh), shard(x - 1, hh), xa_s.at[k, 0], xa_r.at[k, 0], right).wait_recv()
        part = shard_part(x - 1, hh, 0, cut)
        cp = copy(part, part, xa_s.at[k, 2], xa_r.at[k, 2], right)
        cp.start()
        x_copies.append(cp)
        copy(shard(x + 1, hh), shard(x + 1, hh), xa_s.at[k, 1], xa_r.at[k, 1], left).wait_recv()
        part = shard_part(x + 1, hh, cut, 3 - cut)
        cp = copy(part, part, xa_s.at[k, 3], xa_r.at[k, 3], left)
        cp.start()
        x_copies.append(cp)

    def x_finish(hh, k):
        cut = 2 if k == 0 else 1
        part = shard_part(x + 2, hh, 0, cut)
        copy(part, part, xa_s.at[k, 2], xa_r.at[k, 2], right).wait_recv()
        part = shard_part(x + 2, hh, cut, 3 - cut)
        copy(part, part, xa_s.at[k, 3], xa_r.at[k, 3], left).wait_recv()

    x_share(yh, 0)
    sign = jnp.where(q == 0, -1, 1)
    edge = (q == 0) | (q == NQ - 1)
    odd = z % 2
    oh = 1 - yh

    def piece(xx, hh, h, k):
        start = 192 * (2 * ((xx + NX) % NX) + hh) + 96 * h + 48 * k
        return w2.at[pl.ds(pl.multiple_of(start, 16), 48)]

    def send_piece(ref, s, r, to):
        cp = copy(ref, ref, s, r, to)
        cp.start()
        x_copies.append(cp)

    y_copies = []
    for k in range(2):
        for j in (1, 0):
            ref = piece(x, yh, odd, k)
            y_copies.append(copy(ref, ref, ya_s.at[k, j], ya_r.at[k], dev(dy=sign * (j + 1))))

    @pl.when(edge)
    def _():
        for cp in y_copies:
            cp.start()

    up_z, down_z = dev(z_to=(z + 1) % NZ), dev(z_to=(z + NZ - 1) % NZ)

    def z_send(dx, k):
        ref = piece(x + dx, oh, odd, k)
        send_piece(ref, za_s.at[dx, k], za_r.at[dx, k], (up_z, down_z)[k])

    def norm(t0):
        def step(i, _):
            rows = pl.ds(pl.multiple_of(t0 + i * 128, 128), 128)
            v = xin[rows, :].astype(F32)
            s = lax.rsqrt(jnp.mean(v * v, axis=-1, keepdims=True) + 1e-6)
            invr[rows, :] = jnp.broadcast_to(s, (128, 128))
            hc[0, rows, :] = (v * s * (1.0 + gain[...])).astype(BF16)
            hc[1, rows, :] = cin[rows, :]
            return 0

        lax.fori_loop(0, TOK // 128, step, 0)

    norm(mine)
    for k in range(2):
        ref = piece(x, oh, odd, k)
        copy(ref, ref, ya_s.at[k, 0], ya_r.at[k], right).wait_recv()
        for j, to in enumerate((right, left)):
            send_piece(ref, xo_s.at[k, j], xo_r.at[k, j], to)
        z_send(0, k)
    x_forward(yh, 0)
    for cp, ref in zip(acts, (xin, cin)):
        cp.wait()
    for k in range(2):
        for j, dx in enumerate((3, 1)):
            ref = piece(x + dx, oh, odd, k)
            copy(ref, ref, xo_s.at[k, j], xo_r.at[k, j], right).wait_recv()
            if j == k:
                send_piece(ref, xo_s.at[2, k], xo_r.at[2, k], (right, left)[k])
            z_send(dx, k)
    norm(theirs)
    x_finish(yh, 0)
    for k in range(2):
        ref = piece(x + 2, oh, odd, k)
        copy(ref, ref, xo_s.at[2, k], xo_r.at[2, k], right).wait_recv()
        z_send(2, k)
    for dx in (0, 3, 1, 2):
        for k in range(2):
            ref = piece(x + dx, oh, 1 - odd, k)
            copy(ref, ref, za_s.at[dx, k], za_r.at[dx, k], right).wait_recv()
    for cp in x_copies:
        cp.wait_send()

    @pl.when(edge)
    def _():
        for cp in y_copies:
            cp.wait_send()

    def hidden(i, _):
        u, t = i // 4, i % 4
        toks = pl.ds(pl.multiple_of(t * 256, 256), 256)
        hb, cb = hc[0, toks, :], hc[1, toks, :]

        def rows(kind):
            return w2[blocks(8 * kind + 4 * u, 4), :]

        pa = lax.dot_general(rows(0), hb, NT, preferred_element_type=F32)
        pb = lax.dot_general(rows(1), hb, NT, preferred_element_type=F32)
        dz = lax.dot_general(rows(2), cb, NT, preferred_element_type=F32)
        sq = pa * pa
        th = jnp.tanh(GELU_K * (pa + 0.044715 * (sq * pa)))
        half = 0.5 * (1.0 + th)
        gelu = pa * half
        slope = half + (0.5 * GELU_K) * pa * (1.0 - th * th) * (1.0 + (3 * 0.044715) * sq)
        for kind, val in enumerate((slope * (dz * pb), dz * gelu, gelu * pb)):
            at = pl.ds(pl.multiple_of(512 * kind + 256 * u, 256), 256)
            pt[at, toks] = val.astype(BF16)
        return 0

    lax.fori_loop(0, 8, hidden, 0)

    def grad_rows(dx, p):
        xt = (x + dx) % NX
        cols = pl.ds(COLS[p][0], COLS[p][1])
        for i in range(3):
            n = 3 * xt + i
            val = jnp.dot(
                pt[pl.ds(pl.multiple_of(128 * n, 128), 128), :],
                hc[jnp.where(n < 8, 0, 1), :, cols],
                preferred_element_type=F32,
            ).astype(BF16)
            for e in range(2):
                m, j = divmod(2 * i + e, 3)
                g4[2 * xt + m, j, :, cols] = val[64 * e : 64 * (e + 1)]

    def part(m, p):
        return g4.at[m, :, :, pl.ds(COLS[p][0], COLS[p][1])]

    def xbuf(i, p):
        return xr.at[i, :, :, pl.ds(COLS[p][0], COLS[p][1])]

    x_grad, relocs, y_grad = [], [], []

    def x_send(src, i, p, to):
        cp = copy(src, xbuf(i, p), xg_s.at[i, p], xg_r.at[i, p], to)
        cp.start()
        x_grad.append(cp)

    def x_wait(i, p):
        copy(xbuf(i, p), xbuf(i, p), xg_s.at[i, p], xg_r.at[i, p], right).wait_recv()

    pieces = range(len(COLS))
    far, near_r, near_l = (x + 2) % NX, (x + 1) % NX, (x + 3) % NX

    def rows_far(p):
        grad_rows(2, p)
        x_send(part(2 * far, p), 0, p, right)
        x_send(part(2 * far + 1, p), 1, p, left)

    def rows_near(p):
        grad_rows(1, p)
        x_send(part(2 * near_r + 1, p), 2, p, right)
        grad_rows(3, p)
        x_send(part(2 * near_l, p), 3, p, left)
        grad_rows(0, p)

    def x_pass(p):
        cols = pl.ds(COLS[p][0], COLS[p][1])
        for i, m, to in ((0, 2 * near_r, right), (1, 2 * near_l + 1, left)):
            x_wait(i, p)
            tot = g4[m, :, :, cols].astype(F32) + xr[i, :, :, cols].astype(F32)
            g4[m, :, :, cols] = tot.astype(BF16)
            x_send(part(m, p), 4 + i, p, to)

    def x_done(p):
        cols = pl.ds(COLS[p][0], COLS[p][1])
        for i, (one, two) in enumerate(((4, 3), (2, 5))):
            x_wait(two if i == 0 else one, p)
            x_wait(one if i == 0 else two, p)
            tot = g4[2 * x + i, :, :, cols].astype(F32) + xr[one, :, :, cols].astype(F32)
            tot = (tot + xr[two, :, :, cols].astype(F32)).astype(BF16)
            for j in range(3):
                slot = jnp.where(c == 0, (0, 2, 3)[j], (3, 0, 2)[j])
                s2[i, pl.ds(pl.multiple_of(64 * slot, 64), 64), cols] = tot[j]
        cp = copy(
            s2.at[:, pl.ds(192, 64), cols], s2.at[:, pl.ds(64, 64), cols], rl_s.at[p], rl_r.at[p], other
        )
        cp.start()
        relocs.append(cp)

    def y_start(p):
        cols = pl.ds(COLS[p][0], COLS[p][1])
        relocs[p].wait_recv()
        for d in (4, 3, 5, 2, 6, 1, 7):
            yt = (y + d) % NY
            cp = copy(
                s2.at[yt // 4, pl.ds(pl.multiple_of(48 * (yt % 4), 16), 48), cols],
                yr.at[d, :, cols],
                yg_s.at[d, p],
                yg_r.at[d, p],
                dev(dy=d),
            )
            cp.start()
            y_grad.append(cp)

    def dh_rows(t0):
        def step(i, _):
            toks = pl.ds(pl.multiple_of(t0 + i * 256, 256), 256)
            dh[toks, :] = lax.dot_general(
                pt[pl.ds(0, 1024), toks], w2[0:1024, :], TN, preferred_element_type=F32
            )
            return 0

        lax.fori_loop(0, 2, step, 0)

    last = len(COLS) - 1
    rows_far(0)
    rows_near(0)
    for p in range(1, last + 1):
        rows_far(p)
        x_pass(p - 1)
        rows_near(p)
        if p >= 2:
            x_done(p - 2)
            y_start(p - 2)
    if last >= 1:
        x_done(last - 1)
        y_start(last - 1)
    x_pass(last)
    dh_rows(theirs)
    dh_copy = copy(dh.at[pl.ds(theirs, TOK)], dhr, dh_s, dh_r, other)
    dh_copy.start()
    x_done(last)
    y_start(last)
    dh_rows(mine)

    dh_copy.wait()

    def finish_input(i, _):
        loc = pl.ds(pl.multiple_of(i * 128, 128), 128)
        rows = pl.ds(pl.multiple_of(mine + i * 128, 128), 128)
        dn = (dh[rows, :] + dhr[loc, :]) * (1.0 + gain[...])
        s = invr[rows, 0:1]
        n = xin[rows, :].astype(F32) * s
        mean = jnp.mean(dn * n, axis=-1, keepdims=True)
        gin_o[loc, :] = (cin[rows, :].astype(F32) + s * (dn - n * mean)).astype(BF16)
        return 0

    lax.fori_loop(0, TOK // 128, finish_input, 0)

    own = pl.ds(pl.multiple_of(48 * q, 16), 48)
    for p in pieces:
        cols = pl.ds(COLS[p][0], COLS[p][1])
        tot = s2[yh, own, cols].astype(F32)
        for d in range(1, NY):
            copy(
                yr.at[d, :, cols], yr.at[d, :, cols], yg_s.at[d, p], yg_r.at[d, p], right
            ).wait_recv()
            tot = tot + yr[d, :, cols].astype(F32)
        tsum[:, cols] = tot

    zs[...] = jnp.zeros_like(zs)
    for r in range(48):
        blk, jj = divmod(r, 6)
        for w in range(5):
            zs[blk, pl.ds(5 * jj + w, 1), :] = tsum[pl.ds(r, 1), pl.ds(128 * w, 128)]
    zb[...] = zs[...].astype(BF16)
    for e in range(2):
        for qt in range(NQ):
            zt = 2 * q + e
            self = (zt == z) & (q == qt)

            @pl.when(jnp.logical_not(self))
            def _():
                copy(
                    zb.at[e * 4 + qt], zr.at[z], zg_s.at[e * 4 + qt], zg_r.at[z],
                    dev(z_to=zt, y_to=yh * 4 + qt),
                ).start()

            @pl.when(self)
            def _():
                zr[z] = zb[e * 4 + qt]

    tot = jnp.zeros((32, 128), F32)
    for zf in range(NZ):
        self = (z // 2 == q) & (z == zf)

        @pl.when(jnp.logical_not(self))
        def _():
            copy(zr.at[zf], zr.at[zf], zg_s.at[0], zg_r.at[zf], right).wait_recv()

        tot = tot + zr[zf].astype(F32)

    grad = tot[0:30] * (1.0 / 512.0)
    n1 = 0.9 * state[1] + 0.1 * grad
    n2 = 0.95 * state[2] + 0.05 * grad * grad
    nm = state[0] - 0.01 * (n1 / (jnp.sqrt(n2) + 1e-8) + 0.1 * state[0])
    nb[pl.ds(0, 30), :] = nm
    nb[pl.ds(30, 2), :] = jnp.zeros((2, 128), F32)
    nwr[b] = nb[...].astype(BF16)
    new = []
    near_first = [(dz, dq) for dz in range(NZ) for dq in range(NQ) if dz or dq]
    near_first.sort(key=lambda v: (min(v[0], NZ - v[0]) + v[1], v))
    for dz, dq in near_first[::-1]:
        cp = copy(
            nwr.at[b], nwr.at[b], nw_s.at[dz, dq], nw_r.at[dz, dq],
            dev(z_to=(z + dz) % NZ, y_to=yh * 4 + (q + dq) % NQ),
        )
        cp.start()
        new.append(cp)
    for ref, val in ((grad_o, grad), (n1_o, n1), (n2_o, n2), (nm_o, nm)):
        for r in range(30):
            ref[:, pl.ds(128 * r, 128)] = val[r : r + 1]

    for cp in relocs + x_grad + y_grad:
        cp.wait_send()
    for e in range(2):
        for qt in range(NQ):
            self = (2 * q + e == z) & (q == qt)

            @pl.when(jnp.logical_not(self))
            def _():
                copy(zb.at[e * 4 + qt], zr.at[z], zg_s.at[e * 4 + qt], zg_r.at[z], right).wait_send()

    def lay_flat(i):
        rows = nwr[i].astype(F32)
        for r in range(30):
            nw_o[:, pl.ds(pl.multiple_of(3840 * i + 128 * r, 128), 128)] = rows[r : r + 1].astype(BF16)

    lay_flat(b)
    for dz, dq in near_first:
        bf = ((z - dz + NZ) % NZ) * 4 + (q - dq + NQ) % NQ
        copy(nwr.at[bf], nwr.at[bf], nw_s.at[dz, dq], nw_r.at[dz, dq], right).wait_recv()
        lay_flat(bf)
    for cp in new:
        cp.wait_send()


def shards(activations, upstream, norm_gain, weight_shards, master, moment_one, moment_two):
    vm = pl.BlockSpec(memory_space=pltpu.VMEM)
    dma = pltpu.SemaphoreType.DMA
    np_ = len(COLS)
    shape = jax.ShapeDtypeStruct
    gin, grad, nw, nm, n1, n2 = pl.pallas_call(
        mesh_kernel,
        out_shape=[
            shape((TOK, D), BF16),
            shape((1, 3840), F32),
            shape((1, 32 * 3840), BF16),
            shape((1, 3840), F32),
            shape((1, 3840), F32),
            shape((1, 3840), F32),
        ],
        in_specs=[pl.BlockSpec(memory_space=pl.ANY)] * 2 + [vm] * 5,
        out_specs=[vm] * 6,
        scratch_shapes=[
            pltpu.VMEM((3 * BLK, D), F32),
            pltpu.VMEM((BLK, D), BF16),
            pltpu.VMEM((3, 30, 128), F32),
            pltpu.VMEM((32, 32, 128), BF16),
            pltpu.VMEM((2 * TOK, D), BF16),
            pltpu.VMEM((2 * TOK, D), BF16),
            pltpu.VMEM((2, 2 * TOK, D), BF16),
            pltpu.VMEM((24 * BLK, D), BF16),
            pltpu.VMEM((1536, 2 * TOK), BF16),
            pltpu.VMEM((8, 3, BLK, D), BF16),
            pltpu.VMEM((2, 256, D), BF16),
            pltpu.VMEM((6, 3, BLK, D), BF16),
            pltpu.VMEM((NY, 48, D), BF16),
            pltpu.VMEM((48, D), F32),
            pltpu.VMEM((8, 32, 128), F32),
            pltpu.VMEM((8, 32, 128), BF16),
            pltpu.VMEM((NZ, 32, 128), BF16),
            pltpu.VMEM((32, 128), F32),
            pltpu.VMEM((2 * TOK, D), F32),
            pltpu.VMEM((TOK, D), F32),
            pltpu.VMEM((2 * TOK, 128), F32),
            dma((2,)),
            dma((2,)), dma((2,)),
            dma, dma,
            dma((2, 2)), dma((2,)),
            dma((1, 4)), dma((1, 4)),
            dma((3, 2)), dma((3, 2)),
            dma((NX, 2)), dma((NX, 2)),
            dma((np_,)), dma((np_,)),
            dma((6, np_)), dma((6, np_)),
            dma((NY, np_)), dma((NY, np_)),
            dma((8,)), dma((NZ,)),
            dma, dma,
            dma((NZ, NQ)), dma((NZ, NQ)),
        ],
        compiler_params=pltpu.CompilerParams(
            collective_id=0, has_side_effects=True, vmem_limit_bytes=56 * 1024 * 1024
        ),
        name="ffn_backward_adam",
    )(activations, upstream, norm_gain, weight_shards, master, moment_one, moment_two)
    return emit(gin, grad, nw, nm, n1, n2)


def emit_kernel(*refs):
    for src, dst in zip(refs[:6], refs[6:]):
        dst[...] = src[...]


def emit(*arrays):
    vm = pl.BlockSpec(memory_space=pltpu.VMEM)
    return pl.pallas_call(
        emit_kernel,
        out_shape=[jax.ShapeDtypeStruct(v.shape, v.dtype) for v in arrays],
        in_specs=[vm] * 6,
        out_specs=[vm] * 6,
        name="emit",
    )(*arrays)


def solution(mesh):
    own = P(None, ("dpa", "dpb"))
    rows = P(("dpa", "dpb"), None)
    return jax.shard_map(
        shards,
        mesh=mesh,
        in_specs=(rows, rows, P(), P(None, "dpa"), own, own, own),
        out_specs=(rows, own, P(None, "dpa"), own, own, own),
        check_vma=False,
    )
```

```python
import math

import jax
import jax.numpy as jnp
from jax import lax
from jax.experimental import pallas as pl
from jax.experimental.pallas import tpu as pltpu
from jax.sharding import PartitionSpec as P

BF16 = jnp.bfloat16
F32 = jnp.float32
MESH = pl.DeviceIdType.MESH

D = 640
TOK = 512
NX, NY, NZ, NQ = 4, 8, 8, 4
BLK = 64
COLS = ((0, 128), (128, 256), (384, 128), (512, 128))

NT = (((1,), (1,)), ((), ()))
TN = (((0,), (0,)), ((), ()))

GELU_K = math.sqrt(2.0 / math.pi)


def mesh_kernel(
    act, up, gain, wflat, mas, mo1, mo2,
    gin_o, grad_o, nw_o, nm_o, n1_o, n2_o,
    wf, wsh, state, nwr, xin, cin, hc, w2, pt, g4, s2, xr, yr, tsum, zs, zb, zr, nb, dh, dhr, invr,
    ld_s, act_s, act_r, a1_s, a1_r, ya_s, ya_r, xa_s, xa_r, xo_s, xo_r, za_s, za_r, rl_s, rl_r, xg_s, xg_r, yg_s, yg_r,
    zg_s, zg_r, dh_s, dh_r, nw_s, nw_r,
):
    a = lax.axis_index("dpa")
    b = lax.axis_index("dpb")
    x, yh, c = a // 4, (a // 2) % 2, a % 2
    z, q = b // 4, b % 4
    y = yh * 4 + q

    def dev(dx=0, dy=0, z_to=None, y_to=None, c_to=None):
        xt = (x + dx + NX) % NX
        yt = (y + dy + NY) % NY if y_to is None else y_to
        zt = z if z_to is None else z_to
        ct = c if c_to is None else c_to
        return {"dpa": (xt * 2 + yt // 4) * 2 + ct, "dpb": zt * 4 + yt % 4}

    def copy(src, dst, s, r, to):
        return pltpu.make_async_remote_copy(
            src_ref=src, dst_ref=dst, send_sem=s, recv_sem=r, device_id=to, device_id_type=MESH
        )

    barrier = pltpu.get_barrier_semaphore()
    peers = [dev(c_to=1 - c), dev(dx=1), dev(dx=-1)]
    peers += [dev(dy=d) for d in range(1, NY)]
    peers += [dev(z_to=(z + d) % NZ) for d in range(1, NZ)]
    for to in peers:
        pl.semaphore_signal(barrier, inc=1, device_id=to, device_id_type=MESH)

    mine = pl.multiple_of(c * TOK, TOK)
    theirs = pl.multiple_of((1 - c) * TOK, TOK)
    own_t = 3 * (2 * x + yh)

    def blocks(t, n=1):
        return pl.ds(pl.multiple_of(BLK * t, BLK), BLK * n)

    loads = [
        pltpu.make_async_copy(src, dst.at[pl.ds(mine, TOK)], ld_s.at[i])
        for i, (src, dst) in enumerate(((act, xin), (up, cin)))
    ]
    for cp in loads:
        cp.start()
    for r in range(3 * BLK):
        wf[pl.ds(r, 1), :] = wflat[:, pl.ds(D * r, D)].astype(F32)
    w2[blocks(own_t + c)] = wf[0:64].astype(BF16)
    wsh[...] = wf[64:128].astype(BF16)
    w2[blocks(own_t + c + 1)] = wf[128:192].astype(BF16)
    for i, ref in enumerate((mas, mo1, mo2)):
        for r in range(30):
            state[i, pl.ds(r, 1), :] = ref[:, pl.ds(128 * r, 128)]
    pl.semaphore_wait(barrier, len(peers))

    other = dev(c_to=1 - c)
    a1 = copy(wsh, w2.at[blocks(own_t + 2 * c)], a1_s, a1_r, other)
    a1.start()
    acts = [
        copy(ref.at[pl.ds(mine, TOK)], ref.at[pl.ds(mine, TOK)], act_s.at[i], act_r.at[i], other)
        for i, ref in enumerate((xin, cin))
    ]
    for cp, load in zip(acts, loads):
        load.wait()
        cp.start()
    a1.wait()

    def shard(xx, hh):
        return shard_part(xx, hh, 0, 3)

    def shard_part(xx, hh, start, n):
        at = 192 * (2 * ((xx + NX) % NX) + hh) + BLK * start
        return w2.at[pl.ds(pl.multiple_of(at, BLK), BLK * n)]

    left, right = dev(dx=-1), dev(dx=1)
    x_copies = []

    def x_share(hh, k):
        for j, to in enumerate((right, left)):
            cp = copy(shard(x, hh), shard(x, hh), xa_s.at[k, j], xa_r.at[k, j], to)
            cp.start()
            x_copies.append(cp)

    def x_forward(hh, k):
        cut = 2 if k == 0 else 1
        copy(shard(x - 1, hh), shard(x - 1, hh), xa_s.at[k, 0], xa_r.at[k, 0], right).wait_recv()
        part = shard_part(x - 1, hh, 0, cut)
        cp = copy(part, part, xa_s.at[k, 2], xa_r.at[k, 2], right)
        cp.start()
        x_copies.append(cp)
        copy(shard(x + 1, hh), shard(x + 1, hh), xa_s.at[k, 1], xa_r.at[k, 1], left).wait_recv()
        part = shard_part(x + 1, hh, cut, 3 - cut)
        cp = copy(part, part, xa_s.at[k, 3], xa_r.at[k, 3], left)
        cp.start()
        x_copies.append(cp)

    def x_finish(hh, k):
        cut = 2 if k == 0 else 1
        part = shard_part(x + 2, hh, 0, cut)
        copy(part, part, xa_s.at[k, 2], xa_r.at[k, 2], right).wait_recv()
        part = shard_part(x + 2, hh, cut, 3 - cut)
        copy(part, part, xa_s.at[k, 3], xa_r.at[k, 3], left).wait_recv()

    x_share(yh, 0)
    sign = jnp.where(q == 0, -1, 1)
    edge = (q == 0) | (q == NQ - 1)
    odd = z % 2
    oh = 1 - yh

    def piece(xx, hh, h, k):
        start = 192 * (2 * ((xx + NX) % NX) + hh) + 96 * h + 48 * k
        return w2.at[pl.ds(pl.multiple_of(start, 16), 48)]

    def send_piece(ref, s, r, to):
        cp = copy(ref, ref, s, r, to)
        cp.start()
        x_copies.append(cp)

    y_copies = []
    for k in range(2):
        for j in (1, 0):
            ref = piece(x, yh, odd, k)
            y_copies.append(copy(ref, ref, ya_s.at[k, j], ya_r.at[k], dev(dy=sign * (j + 1))))

    @pl.when(edge)
    def _():
        for cp in y_copies:
            cp.start()

    up_z, down_z = dev(z_to=(z + 1) % NZ), dev(z_to=(z + NZ - 1) % NZ)

    def z_send(dx, k):
        ref = piece(x + dx, oh, odd, k)
        send_piece(ref, za_s.at[dx, k], za_r.at[dx, k], (up_z, down_z)[k])

    def norm(t0):
        def step(i, _):
            rows = pl.ds(pl.multiple_of(t0 + i * 128, 128), 128)
            v = xin[rows, :].astype(F32)
            s = lax.rsqrt(jnp.mean(v * v, axis=-1, keepdims=True) + 1e-6)
            invr[rows, :] = jnp.broadcast_to(s, (128, 128))
            hc[0, rows, :] = (v * s * (1.0 + gain[...])).astype(BF16)
            hc[1, rows, :] = cin[rows, :]
            return 0

        lax.fori_loop(0, TOK // 128, step, 0)

    norm(mine)
    for k in range(2):
        ref = piece(x, oh, odd, k)
        copy(ref, ref, ya_s.at[k, 0], ya_r.at[k], right).wait_recv()
        for j, to in enumerate((right, left)):
            send_piece(ref, xo_s.at[k, j], xo_r.at[k, j], to)
        z_send(0, k)
    x_forward(yh, 0)
    for cp, ref in zip(acts, (xin, cin)):
        cp.wait()
    for k in range(2):
        for j, dx in enumerate((3, 1)):
            ref = piece(x + dx, oh, odd, k)
            copy(ref, ref, xo_s.at[k, j], xo_r.at[k, j], right).wait_recv()
            if j == k:
                send_piece(ref, xo_s.at[2, k], xo_r.at[2, k], (right, left)[k])
            z_send(dx, k)
    norm(theirs)
    x_finish(yh, 0)
    for k in range(2):
        ref = piece(x + 2, oh, odd, k)
        copy(ref, ref, xo_s.at[2, k], xo_r.at[2, k], right).wait_recv()
        z_send(2, k)
    for dx in (0, 3, 1, 2):
        for k in range(2):
            ref = piece(x + dx, oh, 1 - odd, k)
            copy(ref, ref, za_s.at[dx, k], za_r.at[dx, k], right).wait_recv()
    for cp in x_copies:
        cp.wait_send()

    @pl.when(edge)
    def _():
        for cp in y_copies:
            cp.wait_send()

    def hidden(i, _):
        u, t = i // 4, i % 4
        toks = pl.ds(pl.multiple_of(t * 256, 256), 256)
        hb, cb = hc[0, toks, :], hc[1, toks, :]

        def rows(kind):
            return w2[blocks(8 * kind + 4 * u, 4), :]

        pa = lax.dot_general(rows(0), hb, NT, preferred_element_type=F32)
        pb = lax.dot_general(rows(1), hb, NT, preferred_element_type=F32)
        dz = lax.dot_general(rows(2), cb, NT, preferred_element_type=F32)
        sq = pa * pa
        th = jnp.tanh(GELU_K * (pa + 0.044715 * (sq * pa)))
        half = 0.5 * (1.0 + th)
        gelu = pa * half
        slope = half + (0.5 * GELU_K) * pa * (1.0 - th * th) * (1.0 + (3 * 0.044715) * sq)
        for kind, val in enumerate((slope * (dz * pb), dz * gelu, gelu * pb)):
            at = pl.ds(pl.multiple_of(512 * kind + 256 * u, 256), 256)
            pt[at, toks] = val.astype(BF16)
        return 0

    lax.fori_loop(0, 8, hidden, 0)

    def grad_rows(dx, p):
        xt = (x + dx) % NX
        cols = pl.ds(COLS[p][0], COLS[p][1])
        for i in range(3):
            n = 3 * xt + i
            val = jnp.dot(
                pt[pl.ds(pl.multiple_of(128 * n, 128), 128), :],
                hc[jnp.where(n < 8, 0, 1), :, cols],
                preferred_element_type=F32,
            ).astype(BF16)
            for e in range(2):
                m, j = divmod(2 * i + e, 3)
                g4[2 * xt + m, j, :, cols] = val[64 * e : 64 * (e + 1)]

    def part(m, p):
        return g4.at[m, :, :, pl.ds(COLS[p][0], COLS[p][1])]

    def xbuf(i, p):
        return xr.at[i, :, :, pl.ds(COLS[p][0], COLS[p][1])]

    x_grad, relocs, y_grad = [], [], []

    def x_send(src, i, p, to):
        cp = copy(src, xbuf(i, p), xg_s.at[i, p], xg_r.at[i, p], to)
        cp.start()
        x_grad.append(cp)

    def x_wait(i, p):
        copy(xbuf(i, p), xbuf(i, p), xg_s.at[i, p], xg_r.at[i, p], right).wait_recv()

    pieces = range(len(COLS))
    far, near_r, near_l = (x + 2) % NX, (x + 1) % NX, (x + 3) % NX

    def rows_far(p):
        grad_rows(2, p)
        x_send(part(2 * far, p), 0, p, right)
        x_send(part(2 * far + 1, p), 1, p, left)

    def rows_near(p):
        grad_rows(1, p)
        x_send(part(2 * near_r + 1, p), 2, p, right)
        grad_rows(3, p)
        x_send(part(2 * near_l, p), 3, p, left)
        grad_rows(0, p)

    def x_pass(p):
        cols = pl.ds(COLS[p][0], COLS[p][1])
        for i, m, to in ((0, 2 * near_r, right), (1, 2 * near_l + 1, left)):
            x_wait(i, p)
            tot = g4[m, :, :, cols].astype(F32) + xr[i, :, :, cols].astype(F32)
            g4[m, :, :, cols] = tot.astype(BF16)
            x_send(part(m, p), 4 + i, p, to)

    def x_done(p):
        cols = pl.ds(COLS[p][0], COLS[p][1])
        for i, (one, two) in enumerate(((4, 3), (2, 5))):
            x_wait(two if i == 0 else one, p)
            x_wait(one if i == 0 else two, p)
            tot = g4[2 * x + i, :, :, cols].astype(F32) + xr[one, :, :, cols].astype(F32)
            tot = (tot + xr[two, :, :, cols].astype(F32)).astype(BF16)
            for j in range(3):
                slot = jnp.where(c == 0, (0, 2, 3)[j], (3, 0, 2)[j])
                s2[i, pl.ds(pl.multiple_of(64 * slot, 64), 64), cols] = tot[j]
        cp = copy(
            s2.at[:, pl.ds(192, 64), cols], s2.at[:, pl.ds(64, 64), cols], rl_s.at[p], rl_r.at[p], other
        )
        cp.start()
        relocs.append(cp)

    def y_start(p):
        cols = pl.ds(COLS[p][0], COLS[p][1])
        relocs[p].wait_recv()
        for d in (4, 3, 5, 2, 6, 1, 7):
            yt = (y + d) % NY
            cp = copy(
                s2.at[yt // 4, pl.ds(pl.multiple_of(48 * (yt % 4), 16), 48), cols],
                yr.at[d, :, cols],
                yg_s.at[d, p],
                yg_r.at[d, p],
                dev(dy=d),
            )
            cp.start()
            y_grad.append(cp)

    def dh_rows(t0):
        def step(i, _):
            toks = pl.ds(pl.multiple_of(t0 + i * 256, 256), 256)
            dh[toks, :] = lax.dot_general(
                pt[pl.ds(0, 1024), toks], w2[0:1024, :], TN, preferred_element_type=F32
            )
            return 0

        lax.fori_loop(0, 2, step, 0)

    rows_far(0)
    rows_near(0)
    rows_far(1)
    x_pass(0)
    rows_near(1)
    rows_far(2)
    x_pass(1)
    rows_near(2)
    x_done(0)
    y_start(0)
    rows_far(3)
    x_pass(2)
    rows_near(3)
    x_done(1)
    y_start(1)
    x_pass(3)
    x_done(2)
    y_start(2)
    dh_rows(theirs)
    dh_copy = copy(dh.at[pl.ds(theirs, TOK)], dhr, dh_s, dh_r, other)
    dh_copy.start()
    x_done(3)
    y_start(3)
    dh_rows(mine)

    dh_copy.wait()

    def finish_input(i, _):
        loc = pl.ds(pl.multiple_of(i * 128, 128), 128)
        rows = pl.ds(pl.multiple_of(mine + i * 128, 128), 128)
        dn = (dh[rows, :] + dhr[loc, :]) * (1.0 + gain[...])
        s = invr[rows, 0:1]
        n = xin[rows, :].astype(F32) * s
        mean = jnp.mean(dn * n, axis=-1, keepdims=True)
        gin_o[loc, :] = (cin[rows, :].astype(F32) + s * (dn - n * mean)).astype(BF16)
        return 0

    lax.fori_loop(0, TOK // 128, finish_input, 0)

    own = pl.ds(pl.multiple_of(48 * q, 16), 48)
    for p in pieces:
        cols = pl.ds(COLS[p][0], COLS[p][1])
        tot = s2[yh, own, cols].astype(F32)
        for d in range(1, NY):
            copy(
                yr.at[d, :, cols], yr.at[d, :, cols], yg_s.at[d, p], yg_r.at[d, p], right
            ).wait_recv()
            tot = tot + yr[d, :, cols].astype(F32)
        tsum[:, cols] = tot

    zs[...] = jnp.zeros_like(zs)
    for r in range(48):
        blk, jj = divmod(r, 6)
        for w in range(5):
            zs[blk, pl.ds(5 * jj + w, 1), :] = tsum[pl.ds(r, 1), pl.ds(128 * w, 128)]
    zb[...] = zs[...].astype(BF16)
    for e in range(2):
        for qt in range(NQ):
            zt = 2 * q + e
            self = (zt == z) & (q == qt)

            @pl.when(jnp.logical_not(self))
            def _():
                copy(
                    zb.at[e * 4 + qt], zr.at[z], zg_s.at[e * 4 + qt], zg_r.at[z],
                    dev(z_to=zt, y_to=yh * 4 + qt),
                ).start()

            @pl.when(self)
            def _():
                zr[z] = zb[e * 4 + qt]

    tot = jnp.zeros((32, 128), F32)
    for zf in range(NZ):
        self = (z // 2 == q) & (z == zf)

        @pl.when(jnp.logical_not(self))
        def _():
            copy(zr.at[zf], zr.at[zf], zg_s.at[0], zg_r.at[zf], right).wait_recv()

        tot = tot + zr[zf].astype(F32)

    grad = tot[0:30] * (1.0 / 512.0)
    n1 = 0.9 * state[1] + 0.1 * grad
    n2 = 0.95 * state[2] + 0.05 * grad * grad
    nm = state[0] - 0.01 * (n1 / (jnp.sqrt(n2) + 1e-8) + 0.1 * state[0])
    nb[pl.ds(0, 30), :] = nm
    nb[pl.ds(30, 2), :] = jnp.zeros((2, 128), F32)
    nwr[b] = nb[...].astype(BF16)
    new = []
    near_first = [(dz, dq) for dz in range(NZ) for dq in range(NQ) if dz or dq]
    near_first.sort(key=lambda v: (min(v[0], NZ - v[0]) + v[1], v))
    for dz, dq in near_first[::-1]:
        cp = copy(
            nwr.at[b], nwr.at[b], nw_s.at[dz, dq], nw_r.at[dz, dq],
            dev(z_to=(z + dz) % NZ, y_to=yh * 4 + (q + dq) % NQ),
        )
        cp.start()
        new.append(cp)
    for ref, val in ((grad_o, grad), (n1_o, n1), (n2_o, n2), (nm_o, nm)):
        for r in range(30):
            ref[:, pl.ds(128 * r, 128)] = val[r : r + 1]

    for cp in relocs + x_grad + y_grad:
        cp.wait_send()
    for e in range(2):
        for qt in range(NQ):
            self = (2 * q + e == z) & (q == qt)

            @pl.when(jnp.logical_not(self))
            def _():
                copy(zb.at[e * 4 + qt], zr.at[z], zg_s.at[e * 4 + qt], zg_r.at[z], right).wait_send()

    def lay_flat(i):
        rows = nwr[i].astype(F32)
        for r in range(30):
            nw_o[:, pl.ds(pl.multiple_of(3840 * i + 128 * r, 128), 128)] = rows[r : r + 1].astype(BF16)

    lay_flat(b)
    for dz, dq in near_first:
        bf = ((z - dz + NZ) % NZ) * 4 + (q - dq + NQ) % NQ
        copy(nwr.at[bf], nwr.at[bf], nw_s.at[dz, dq], nw_r.at[dz, dq], right).wait_recv()
        lay_flat(bf)
    for cp in new:
        cp.wait_send()


def shards(activations, upstream, norm_gain, weight_shards, master, moment_one, moment_two):
    vm = pl.BlockSpec(memory_space=pltpu.VMEM)
    dma = pltpu.SemaphoreType.DMA
    np_ = len(COLS)
    shape = jax.ShapeDtypeStruct
    gin, grad, nw, nm, n1, n2 = pl.pallas_call(
        mesh_kernel,
        out_shape=[
            shape((TOK, D), BF16),
            shape((1, 3840), F32),
            shape((1, 32 * 3840), BF16),
            shape((1, 3840), F32),
            shape((1, 3840), F32),
            shape((1, 3840), F32),
        ],
        in_specs=[pl.BlockSpec(memory_space=pl.ANY)] * 2 + [vm] * 5,
        out_specs=[vm] * 6,
        scratch_shapes=[
            pltpu.VMEM((3 * BLK, D), F32),
            pltpu.VMEM((BLK, D), BF16),
            pltpu.VMEM((3, 30, 128), F32),
            pltpu.VMEM((32, 32, 128), BF16),
            pltpu.VMEM((2 * TOK, D), BF16),
            pltpu.VMEM((2 * TOK, D), BF16),
            pltpu.VMEM((2, 2 * TOK, D), BF16),
            pltpu.VMEM((24 * BLK, D), BF16),
            pltpu.VMEM((1536, 2 * TOK), BF16),
            pltpu.VMEM((8, 3, BLK, D), BF16),
            pltpu.VMEM((2, 256, D), BF16),
            pltpu.VMEM((6, 3, BLK, D), BF16),
            pltpu.VMEM((NY, 48, D), BF16),
            pltpu.VMEM((48, D), F32),
            pltpu.VMEM((8, 32, 128), F32),
            pltpu.VMEM((8, 32, 128), BF16),
            pltpu.VMEM((NZ, 32, 128), BF16),
            pltpu.VMEM((32, 128), F32),
            pltpu.VMEM((2 * TOK, D), F32),
            pltpu.VMEM((TOK, D), F32),
            pltpu.VMEM((2 * TOK, 128), F32),
            dma((2,)),
            dma((2,)), dma((2,)),
            dma, dma,
            dma((2, 2)), dma((2,)),
            dma((1, 4)), dma((1, 4)),
            dma((3, 2)), dma((3, 2)),
            dma((NX, 2)), dma((NX, 2)),
            dma((np_,)), dma((np_,)),
            dma((6, np_)), dma((6, np_)),
            dma((NY, np_)), dma((NY, np_)),
            dma((8,)), dma((NZ,)),
            dma, dma,
            dma((NZ, NQ)), dma((NZ, NQ)),
        ],
        compiler_params=pltpu.CompilerParams(
            collective_id=0, has_side_effects=True, vmem_limit_bytes=56 * 1024 * 1024
        ),
        name="ffn_backward_adam",
    )(activations, upstream, norm_gain, weight_shards, master, moment_one, moment_two)
    return emit(gin, grad, nw, nm, n1, n2)


def emit_kernel(*refs):
    for src, dst in zip(refs[:6], refs[6:]):
        dst[...] = src[...]


def emit(*arrays):
    vm = pl.BlockSpec(memory_space=pltpu.VMEM)
    return pl.pallas_call(
        emit_kernel,
        out_shape=[jax.ShapeDtypeStruct(v.shape, v.dtype) for v in arrays],
        in_specs=[vm] * 6,
        out_specs=[vm] * 6,
        name="emit",
    )(*arrays)


def solution(mesh):
    own = P(None, ("dpa", "dpb"))
    rows = P(("dpa", "dpb"), None)
    return jax.shard_map(
        shards,
        mesh=mesh,
        in_specs=(rows, rows, P(), P(None, "dpa"), own, own, own),
        out_specs=(rows, own, P(None, "dpa"), own, own, own),
        check_vma=False,
    )
```
